32 devices in a mesh: groups: 2 (over y), batch: 4 (over z), heads: 4 (over x, core).
Axes of the slice: x: 2, y: 2, z: 4, core: 2. Of those that a mesh axis runs over, the one named last changes fastest.
Arguments:
- tokens: bfloat16 [768, 4096], P(('groups', 'batch')), parts along dimension 0, may hold values from -6 to 6
- query_weight: bfloat16 [16, 4096, 128], P('heads', 'batch'), may hold values from -0.09375 to 0.09375
- keys: bfloat16 [4, 768, 128], P('heads', ('groups', 'batch')), parts along dimension 1, may hold values from -48 to 48
- values: bfloat16 [4, 768, 128], P('heads', ('groups', 'batch')), parts along dimension 1, may hold values from -6 to 6
- segment_ids: int32 [768], P(('groups', 'batch')), parts along dimension 0, may hold values from 0 to 1, as said below
- out_weight: bfloat16 [16, 4096, 128], P('heads', 'batch'), may hold values from -1.5 to 1.5
Outputs:
- mixed: bfloat16 [768, 4096], P(('groups', 'batch'), 'heads'), parts along dimension 0
The draws below stay inside these ranges and needn't reach their ends.
There are 2 independent parts, one for each index of `groups`. The reference program is written for one: setup_inputs(seed, part) draws one part's arguments, and reference() takes and returns one part's arrays. A program takes and returns all parts, laid end to end along the dimension named above; an argument that names none is the same for every part. Nothing has to cross between parts.
Inputs may be any that keep to these rules, and one draw needn't show every extreme that they name: `segment_ids`: two sequences in token order, each of at least 96 tokens.
All inputs are finite; a program needn't handle non-finite values.
Results may differ from the reference program's by a relative error of at most 0.0086.
Values may be sent and summed in bfloat16 or wider, within the bound.
A program may use at most 64 MiB of HBM per device.

```python
import jax
import jax.numpy as jnp
from jax import lax

D = 4096
HD = 128
GROUP = 4
KV_HEADS = 4
HEADS = 16
TOKENS = 384


def draw_keys(key, part):
    key = jax.random.fold_in(key, 11)
    base_key = jax.random.fold_in(key, 0)
    base = jax.random.normal(base_key, (KV_HEADS, TOKENS, HD), jnp.float32)
    return jnp.clip(base * 1.2, -6.0, 6.0).astype(jnp.bfloat16)


def draw_segment_ids(key, part):
    key = jax.random.fold_in(key, 23)
    first_len = jax.random.randint(key, (), TOKENS // 4, TOKENS * 3 // 4 + 1, jnp.int32)
    places = jnp.arange(TOKENS, dtype=jnp.int32)
    return jnp.where(places >= first_len, 1, 0).astype(jnp.int32)


def level_of(stream_key, shape, pieces, low, high):
    factor_of = 1.0
    for axis_at, parts in pieces:
        heights = jax.random.uniform(jax.random.fold_in(jax.random.fold_in(stream_key, 6), axis_at), (parts,), jnp.float32, low / len(pieces), high / len(pieces))
        factor_of = factor_of * jnp.repeat(jnp.exp(heights), shape[axis_at] // parts).reshape((-1,) + (1,) * (len(shape) - 1 - axis_at))
    return factor_of


def gaussian(rng, extent, width, bound, pieces=(), held_as=jnp.bfloat16):
    entries = jax.random.normal(rng, extent, jnp.float32) * width
    if len(pieces) > 0:
        entries = level_of(rng, extent, pieces, -0.22, 0.18) * entries
    return jnp.clip(entries, min=-bound, max=bound).astype(held_as)


def setup_inputs(seed: int = 0, part: int = 0) -> dict:
    streams_of = jax.random.split(jax.random.key(seed), 7)
    part_keys = jax.random.split(jax.random.fold_in(streams_of[6], part), 7)
    tokens = gaussian(part_keys[0], (TOKENS, D), 1.0, 6.0, ((0, 4),))
    query_weight = gaussian(streams_of[1], (HEADS, D, HD), D ** -0.5, 0.09375, ((0, 4), (1, 4)))
    keys = draw_keys(jax.random.fold_in(jax.random.fold_in(streams_of[6], part), 71), part)
    values = gaussian(part_keys[3], (KV_HEADS, TOKENS, HD), 1.0, 6.0, ((0, 4), (1, 4)))
    segment_ids = draw_segment_ids(jax.random.fold_in(jax.random.fold_in(streams_of[6], part), 71), part)
    out_weight = gaussian(streams_of[5], (HEADS, D, HD), (HD // 8) ** -0.5, 1.5, ((0, 4), (1, 4)))
    return dict(tokens=tokens, query_weight=query_weight, keys=keys, values=values, segment_ids=segment_ids, out_weight=out_weight)


def one_head(query_w, key_h, value_h, out_w, tokens, segment_ids):
    query = jnp.dot(tokens, query_w, preferred_element_type=jnp.float32).astype(jnp.bfloat16)
    scores = jnp.dot(query.astype(jnp.float32), key_h.astype(jnp.float32).T, precision=lax.Precision.HIGHEST)
    scores = scores / jnp.sqrt(jnp.float32(HD))
    places = jnp.arange(TOKENS, dtype=jnp.int32)
    keep = (segment_ids[None, :] == segment_ids[:, None]) & (places[None, :] <= places[:, None])
    top = lax.optimization_barrier(jnp.max(jnp.where(keep, scores, -jnp.inf), axis=1, keepdims=True))
    weights = jnp.where(keep, jnp.exp(scores - top), jnp.float32(0.0))
    total = lax.optimization_barrier(jnp.sum(weights, axis=1, keepdims=True))
    attended = jnp.dot(weights, value_h.astype(jnp.float32), precision=lax.Precision.HIGHEST) / total
    attended = attended.astype(jnp.bfloat16)
    return jnp.dot(attended, out_w.T, preferred_element_type=jnp.float32)

def reference(tokens, query_weight, keys, values, segment_ids, out_weight):

    def step(carry, index):
        shared = index // GROUP
        term = one_head(query_weight[index], keys[shared], values[shared], out_weight[index], tokens, segment_ids)
        return (carry + term, None)
    start = jnp.zeros((TOKENS, D), jnp.float32)
    total, unused = lax.scan(step, start, jnp.arange(HEADS, dtype=jnp.int32))
    return total.astype(jnp.bfloat16)
```

```python
import functools

import jax
import jax.numpy as jnp
from jax import lax
from jax.experimental import pallas as pl
from jax.experimental.pallas import tpu as pltpu
from jax.sharding import PartitionSpec as P

MESH = pl.DeviceIdType.MESH


def flip(index, mask):
    bit = 1
    while bit <= mask:
        if mask & bit:
            index = index + bit - 2 * bit * lax.rem(lax.div(index, bit), 2)
        bit *= 2
    return index


def kernel(
    tokens,
    query_weight,
    keys,
    values,
    segments,
    out_weight,
    out,
    w_query,
    w_out,
    token_block,
    partial_out,
    partial_in,
    key_all,
    value_all,
    segment_all,
    attended_all,
    core_out,
    core_in,
    chip_out,
    chip_in,
    final,
    load_sem,
    token_send,
    token_recv,
    share_send,
    share_recv,
    key_send,
    key_recv,
    value_send,
    value_recv,
    segment_send,
    segment_recv,
    partial_send,
    partial_recv,
    attended_send,
    attended_recv,
    core_send,
    core_recv,
    chip_send,
    chip_recv,
    final_send,
    final_recv,
):
    rows, model = tokens.shape
    local_heads, depth, head_size = query_weight.shape
    wide = local_heads * head_size
    plane = lax.axis_index("batch")
    head = lax.axis_index("heads")
    others = (1, 2, 3)
    bf16, f32 = jnp.bfloat16, jnp.float32

    def remote(src, dst, send, recv, **device):
        return pltpu.make_async_remote_copy(
            src_ref=src,
            dst_ref=dst,
            send_sem=send,
            recv_sem=recv,
            device_id=device,
            device_id_type=MESH,
        )

    own_tokens = pltpu.make_async_copy(
        tokens.at[:, pl.ds(pl.multiple_of(plane * depth, depth), depth)],
        token_block.at[0],
        load_sem.at[0],
    )
    own_keys = pltpu.make_async_copy(keys.at[0], key_all.at[plane], load_sem.at[1])
    own_values = pltpu.make_async_copy(values.at[0], value_all.at[plane], load_sem.at[2])
    query_loads = [
        pltpu.make_async_copy(
            query_weight.at[i], w_query.at[:, pl.ds(i * head_size, head_size)], load_sem.at[3 + i]
        )
        for i in range(local_heads)
    ]
    out_loads = [
        pltpu.make_async_copy(
            out_weight.at[i],
            w_out.at[:, pl.ds(i * head_size, head_size)],
            load_sem.at[3 + local_heads + i],
        )
        for i in range(local_heads)
    ]
    for load in [*query_loads, own_tokens, own_keys, own_values, *out_loads]:
        load.start()
    segment_all[plane] = jnp.zeros(segment_all.shape[1:], jnp.int32)
    segment_all[plane, 0:1, 0:rows] = segments[...]

    barrier = pltpu.get_barrier_semaphore()
    for d in others:
        pl.semaphore_signal(
            barrier, inc=1, device_id={"batch": flip(plane, d)}, device_id_type=MESH
        )
        pl.semaphore_signal(barrier, inc=1, device_id={"heads": flip(head, d)}, device_id_type=MESH)

    @pl.when(plane != head)
    def _():
        pl.semaphore_signal(
            barrier, inc=1, device_id={"batch": head, "heads": plane}, device_id_type=MESH
        )
        pl.semaphore_wait(barrier, 2 * len(others) + 1)

    @pl.when(plane == head)
    def _():
        pl.semaphore_wait(barrier, 2 * len(others))

    share = depth // (1 + len(SHARE))
    my_share = lax.rem(head, 1 + len(SHARE))
    token_copies, share_copies, key_copies, value_copies, segment_copies = {}, {}, {}, {}, {}
    mine = pl.ds(pl.multiple_of(my_share * share, share), share)
    for d in (2, 3, 1):
        peer = flip(plane, d)
        token_copies[d] = remote(
            tokens.at[:, pl.ds(pl.multiple_of(peer * depth + my_share * share, share), share)],
            token_block.at[d, :, mine],
            token_send.at[d],
            token_recv.at[d],
            batch=peer,
        )
        token_copies[d].start()

    own_keys.wait()
    own_values.wait()

    def send_keys():
        for d in others:
            peer = flip(plane, d)
            key_copies[d] = remote(
                key_all.at[plane], key_all.at[plane], key_send.at[d], key_recv.at[d], batch=peer
            )
            value_copies[d] = remote(
                value_all.at[plane],
                value_all.at[plane],
                value_send.at[d],
                value_recv.at[d],
                batch=peer,
            )
            segment_copies[d] = remote(
                segment_all.at[plane],
                segment_all.at[plane],
                segment_send.at[d],
                segment_recv.at[d],
                batch=peer,
            )
            for copy in (key_copies[d], value_copies[d], segment_copies[d]):
                copy.start()

    for load in query_loads:
        load.wait()
    own_tokens.wait()
    query = jnp.dot(token_block[0], w_query[...], preferred_element_type=f32)

    def forward(d):
        token_copies[d].wait_recv()
        for s, mask in enumerate(SHARE):
            share_copies[d, s] = remote(
                token_block.at[d, :, mine],
                token_block.at[d, :, mine],
                share_send.at[d, s],
                share_recv.at[d, s],
                heads=flip(head, mask),
            )
            share_copies[d, s].start()

    partial_copies = {}
    forward(1)
    forward(2)
    for d in others:
        for s in range(len(SHARE)):
            share_copies[d, s].wait_recv()
        if d == 1:
            forward(3)
        partial_out[d] = jnp.dot(token_block[d], w_query[...], preferred_element_type=f32).astype(
            bf16
        )
        partial_copies[d] = remote(
            partial_out.at[d],
            partial_in.at[d],
            partial_send.at[d],
            partial_recv.at[d],
            batch=flip(plane, d),
        )
        partial_copies[d].start()
        if d == 1:
            send_keys()

    for d in others:
        segment_copies[d].wait_recv()
    count = segment_all.shape[0]
    row_at = lax.broadcasted_iota(jnp.int32, (rows, rows), 0)
    column_at = lax.broadcasted_iota(jnp.int32, (rows, rows), 1)
    own = segment_all[plane, 0:1, 0:rows]
    row_segment = jnp.sum(
        jnp.where(row_at == column_at, jnp.broadcast_to(own, (rows, rows)), 0),
        axis=1,
        keepdims=True,
    )
    segment_row = jnp.concatenate([segment_all[p, 0:1, 0:rows] for p in range(count)], axis=1)
    places = lax.broadcasted_iota(jnp.int32, (rows, count * rows), 1)
    row_places = lax.broadcasted_iota(jnp.int32, (rows, count * rows), 0) + plane * rows
    keep = (segment_row == row_segment) & (places <= row_places)

    for d in others:
        key_copies[d].wait_recv()
        value_copies[d].wait_recv()
    key_block = jnp.concatenate([key_all[p] for p in range(count)], axis=0)
    value_block = jnp.concatenate([value_all[p] for p in range(count)], axis=0)
    for d in others:
        partial_copies[d].wait_recv()
        query = query + partial_in[d].astype(f32)
    query = query.astype(bf16)
    factor = 1.0 / (head_size**0.5)
    attended = []
    for i in range(local_heads):
        scores = (
            lax.dot_general(
                query[:, i * head_size : (i + 1) * head_size],
                key_block,
                (((1,), (1,)), ((), ())),
                preferred_element_type=f32,
            )
            * factor
        )
        top = jnp.max(jnp.where(keep, scores, -1e30), axis=1, keepdims=True)
        weights = jnp.where(keep, jnp.exp(scores - top), 0.0)
        total = jnp.sum(weights, axis=1, keepdims=True)
        gathered = jnp.dot(weights.astype(bf16), value_block, preferred_element_type=f32)
        attended.append((gathered / total).astype(bf16))
    attended_all[plane] = jnp.concatenate(attended, axis=1)

    attended_copies = {}
    for d in (2, 3, 1):
        attended_copies[d] = remote(
            attended_all.at[plane],
            attended_all.at[plane],
            attended_send.at[d],
            attended_recv.at[d],
            batch=flip(plane, d),
        )
        attended_copies[d].start()
    for load in out_loads:
        load.wait()
    for d in others:
        attended_copies[d].wait_recv()

    def product(target):
        return lax.dot_general(
            attended_all[target],
            w_out[...],
            (((1,), (1,)), ((), ())),
            preferred_element_type=f32,
        )

    core_copies = {}
    for slot, mask in ((1, 3), (0, 1)):
        core_out[slot] = product(flip(head, mask)).astype(bf16)
        core_copies[slot] = remote(
            core_out.at[slot],
            core_in.at[slot],
            core_send.at[slot],
            core_recv.at[slot],
            heads=flip(head, 1),
        )
        core_copies[slot].start()
    far = product(flip(head, 2))
    core_copies[1].wait_recv()
    chip_out[...] = (far + core_in[1].astype(f32)).astype(bf16)
    chip_copy = remote(chip_out, chip_in, chip_send, chip_recv, heads=flip(head, 2))
    chip_copy.start()
    near = product(head)
    core_copies[0].wait_recv()
    near = near + core_in[0].astype(f32)
    chip_copy.wait_recv()
    final[...] = (near + chip_in[...].astype(f32)).astype(bf16)

    @pl.when(plane != head)
    def _():
        final_copy = remote(final, out, final_send, final_recv, batch=head, heads=plane)
        final_copy.start()
        final_copy.wait()

    @pl.when(plane == head)
    def _():
        final_copy = pltpu.make_async_copy(final, out, final_send)
        final_copy.start()
        final_copy.wait()

    for copies in (
        token_copies,
        share_copies,
        key_copies,
        value_copies,
        segment_copies,
        partial_copies,
        attended_copies,
        core_copies,
    ):
        for copy in copies.values():
            copy.wait_send()
    chip_copy.wait_send()


SHARE = (1,)


def move_activations(tokens, query_weight, keys, values, segment_ids, out_weight):
    rows, model = tokens.shape
    local_heads, depth, head_size = query_weight.shape
    wide = local_heads * head_size
    count = model // depth
    bf16, dma = jnp.bfloat16, pltpu.SemaphoreType.DMA
    anywhere = pl.BlockSpec(memory_space=pl.ANY)
    scratch = [
        pltpu.VMEM((depth, wide), bf16),
        pltpu.VMEM((depth, wide), bf16),
        pltpu.VMEM((count, rows, depth), bf16),
        pltpu.VMEM((count, rows, wide), bf16),
        pltpu.VMEM((count, rows, wide), bf16),
        pltpu.VMEM((count, rows, head_size), bf16),
        pltpu.VMEM((count, rows, head_size), bf16),
        pltpu.VMEM((count, 8, 128), jnp.int32),
        pltpu.VMEM((count, rows, wide), bf16),
        pltpu.VMEM((2, rows, depth), bf16),
        pltpu.VMEM((2, rows, depth), bf16),
        pltpu.VMEM((rows, depth), bf16),
        pltpu.VMEM((rows, depth), bf16),
        pltpu.VMEM((rows, depth), bf16),
        dma((3 + 2 * local_heads,)),
        dma((count,)),
        dma((count,)),
        dma((count, len(SHARE))),
        dma((count, len(SHARE))),
        *[dma((count,)) for _ in range(10)],
        dma((2,)),
        dma((2,)),
        *[dma for _ in range(4)],
    ]
    return pl.pallas_call(
        kernel,
        out_shape=jax.ShapeDtypeStruct((rows, depth), bf16),
        in_specs=[
            anywhere,
            anywhere,
            anywhere,
            anywhere,
            pl.BlockSpec(memory_space=pltpu.VMEM),
            anywhere,
        ],
        out_specs=anywhere,
        scratch_shapes=scratch,
        compiler_params=pltpu.CompilerParams(
            collective_id=0, has_side_effects=True, vmem_limit_bytes=32 * 1024 * 1024
        ),
        cost_estimate=pl.CostEstimate(
            flops=4 * count * rows * depth * wide + 4 * local_heads * count * rows * rows * head_size,
            bytes_accessed=4 * depth * wide + 4 * rows * model,
            transcendentals=local_heads * count * rows * rows,
        ),
    )(tokens, query_weight, keys, values, segment_ids[None, :], out_weight)


def gather_weights(tokens, query_weight, keys, values, segment_ids, out_weight):
    rows = tokens.shape[0]
    head_size = query_weight.shape[2]
    local_heads = query_weight.shape[0]
    kv_local = keys.shape[0]
    sharing = local_heads // kv_local
    first = lax.axis_index("batch") * rows
    places = first + jnp.arange(rows, dtype=jnp.int32)
    query_places = jnp.tile(places, sharing)
    query_segments = jnp.tile(segment_ids, sharing)
    query = jnp.einsum(
        "tc,hcd->htd",
        tokens,
        lax.all_gather(query_weight, "batch", axis=1, tiled=True),
        preferred_element_type=jnp.float32,
    ).astype(jnp.bfloat16)
    query = query.reshape(kv_local, sharing * rows, head_size)
    factor = 1.0 / jnp.sqrt(jnp.float32(head_size))
    begin = (
        jnp.full((kv_local, sharing * rows), -1e30, jnp.float32),
        jnp.zeros((kv_local, sharing * rows), jnp.float32),
        jnp.zeros((kv_local, sharing * rows, head_size), jnp.float32),
    )
    key_piece = lax.all_gather(keys, "batch", axis=1, tiled=True)
    value_piece = lax.all_gather(values, "batch", axis=1, tiled=True)
    segment_piece = lax.all_gather(segment_ids[None, :], "batch", axis=1, tiled=True)
    count = key_piece.shape[1]
    width = 4
    block = width * rows

    def inner(state, number):
        running, total, gathered = state
        offset = number * block
        key_block = lax.dynamic_slice_in_dim(key_piece, offset, block, 1)
        value_block = lax.dynamic_slice_in_dim(value_piece, offset, block, 1)
        segment_block = lax.dynamic_slice_in_dim(segment_piece[0], offset, block, 0)
        scores = (
            jnp.einsum("gqd,gkd->gqk", query, key_block, preferred_element_type=jnp.float32)
            * factor
        )
        key_places = offset + jnp.arange(block, dtype=jnp.int32)
        keep = (segment_block[None, :] == query_segments[:, None]) & (
            key_places[None, :] <= query_places[:, None]
        )
        block_top = jnp.max(jnp.where(keep[None], scores, jnp.float32(-1e30)), axis=2)
        newer = jnp.maximum(running, block_top)
        weights = jnp.where(keep[None], jnp.exp(scores - newer[:, :, None]), jnp.float32(0.0))
        shrink = jnp.exp(running - newer)
        total = total * shrink + jnp.sum(weights, axis=2)
        gathered = gathered * shrink[:, :, None] + jnp.einsum(
            "gqk,gkd->gqd",
            weights,
            value_block.astype(jnp.float32),
            precision=lax.Precision.HIGHEST,
        )
        return ((newer, total, gathered), None)

    result, unused = lax.scan(inner, begin, jnp.arange(count // block, dtype=jnp.int32))
    running, total, gathered = result
    attended = (
        (gathered / total[:, :, None]).astype(jnp.bfloat16).reshape(local_heads, rows, head_size)
    )
    terms = jnp.einsum(
        "htd,hcd->tc",
        attended,
        lax.all_gather(out_weight, "batch", axis=1, tiled=True),
        preferred_element_type=jnp.float32,
    )
    return lax.psum_scatter(terms, "heads", scatter_dimension=1, tiled=True).astype(jnp.bfloat16)


def solution(mesh):
    batch, heads = mesh.shape["batch"], mesh.shape["heads"]

    def on_device(tokens, query_weight, keys, values, segment_ids, out_weight):
        rows, model = tokens.shape
        local_heads, depth, head_size = query_weight.shape
        wide = local_heads * head_size
        weights = 2 * model * wide
        activations = batch * rows * (depth + 3 * wide + depth)
        plan = move_activations if batch == heads == 4 and activations < weights else gather_weights
        return plan(tokens, query_weight, keys, values, segment_ids, out_weight)

    return jax.shard_map(
        on_device,
        mesh=mesh,
        in_specs=(
            P(("groups", "batch"), None),
            P("heads", "batch", None),
            P("heads", ("groups", "batch"), None),
            P("heads", ("groups", "batch"), None),
            P(("groups", "batch")),
            P("heads", "batch", None),
        ),
        out_specs=P(("groups", "batch"), "heads"),
        check_vma=False,
    )
```

```python
import functools

import jax
import jax.numpy as jnp
from jax import lax
from jax.experimental import pallas as pl
from jax.experimental.pallas import tpu as pltpu
from jax.sharding import PartitionSpec as P

MESH = pl.DeviceIdType.MESH


def flip(index, mask):
    bit = 1
    while bit <= mask:
        if mask & bit:
            index = index + bit - 2 * bit * lax.rem(lax.div(index, bit), 2)
        bit *= 2
    return index


def kernel(
    tokens,
    query_weight,
    keys,
    values,
    segments,
    out_weight,
    out,
    w_query,
    w_out,
    token_block,
    partial_out,
    partial_in,
    key_all,
    value_all,
    segment_all,
    attended_all,
    core_out,
    core_in,
    chip_out,
    chip_in,
    final,
    load_sem,
    token_send,
    token_recv,
    share_send,
    share_recv,
    key_send,
    key_recv,
    value_send,
    value_recv,
    segment_send,
    segment_recv,
    partial_send,
    partial_recv,
    attended_send,
    attended_recv,
    core_send,
    core_recv,
    chip_send,
    chip_recv,
    final_send,
    final_recv,
):
    rows, model = tokens.shape
    local_heads, depth, head_size = query_weight.shape
    wide = local_heads * head_size
    plane = lax.axis_index("batch")
    head = lax.axis_index("heads")
    others = (1, 2, 3)
    bf16, f32 = jnp.bfloat16, jnp.float32

    def remote(src, dst, send, recv, **device):
        return pltpu.make_async_remote_copy(
            src_ref=src,
            dst_ref=dst,
            send_sem=send,
            recv_sem=recv,
            device_id=device,
            device_id_type=MESH,
        )

    own_tokens = pltpu.make_async_copy(
        tokens.at[:, pl.ds(pl.multiple_of(plane * depth, depth), depth)],
        token_block.at[0],
        load_sem.at[0],
    )
    own_keys = pltpu.make_async_copy(keys.at[0], key_all.at[plane], load_sem.at[1])
    own_values = pltpu.make_async_copy(values.at[0], value_all.at[plane], load_sem.at[2])
    query_loads = [
        pltpu.make_async_copy(
            query_weight.at[i], w_query.at[:, pl.ds(i * head_size, head_size)], load_sem.at[3 + i]
        )
        for i in range(local_heads)
    ]
    out_loads = [
        pltpu.make_async_copy(
            out_weight.at[i],
            w_out.at[:, pl.ds(i * head_size, head_size)],
            load_sem.at[3 + local_heads + i],
        )
        for i in range(local_heads)
    ]
    for load in [*query_loads, own_tokens, own_keys, own_values, *out_loads]:
        load.start()
    segment_all[plane] = jnp.zeros(segment_all.shape[1:], jnp.int32)
    segment_all[plane, 0:1, 0:rows] = segments[...]

    barrier = pltpu.get_barrier_semaphore()
    for d in others:
        pl.semaphore_signal(
            barrier, inc=1, device_id={"batch": flip(plane, d)}, device_id_type=MESH
        )
        pl.semaphore_signal(barrier, inc=1, device_id={"heads": flip(head, d)}, device_id_type=MESH)

    @pl.when(plane != head)
    def _():
        pl.semaphore_signal(
            barrier, inc=1, device_id={"batch": head, "heads": plane}, device_id_type=MESH
        )
        pl.semaphore_wait(barrier, 2 * len(others) + 1)

    @pl.when(plane == head)
    def _():
        pl.semaphore_wait(barrier, 2 * len(others))

    share = depth // (1 + len(SHARE))
    my_share = lax.rem(head, 1 + len(SHARE))
    token_copies, share_copies, key_copies, value_copies, segment_copies = {}, {}, {}, {}, {}
    partial_copies, attended_copies, core_copies = {}, {}, {}

    def drain():
        for copies in (
            token_copies,
            share_copies,
            key_copies,
            value_copies,
            segment_copies,
            partial_copies,
            attended_copies,
            core_copies,
        ):
            for copy in copies.values():
                copy.wait_send()

    mine = pl.ds(pl.multiple_of(my_share * share, share), share)
    for d in (2, 3, 1):
        peer = flip(plane, d)
        token_copies[d] = remote(
            tokens.at[:, pl.ds(pl.multiple_of(peer * depth + my_share * share, share), share)],
            token_block.at[d, :, mine],
            token_send.at[d],
            token_recv.at[d],
            batch=peer,
        )
        token_copies[d].start()

    own_keys.wait()
    own_values.wait()

    def send_keys():
        for d in others:
            peer = flip(plane, d)
            key_copies[d] = remote(
                key_all.at[plane], key_all.at[plane], key_send.at[d], key_recv.at[d], batch=peer
            )
            value_copies[d] = remote(
                value_all.at[plane],
                value_all.at[plane],
                value_send.at[d],
                value_recv.at[d],
                batch=peer,
            )
            segment_copies[d] = remote(
                segment_all.at[plane],
                segment_all.at[plane],
                segment_send.at[d],
                segment_recv.at[d],
                batch=peer,
            )
            for copy in (key_copies[d], value_copies[d], segment_copies[d]):
                copy.start()

    for load in query_loads:
        load.wait()
    own_tokens.wait()
    query = jnp.dot(token_block[0], w_query[...], preferred_element_type=f32)

    def forward(d):
        token_copies[d].wait_recv()
        for s, mask in enumerate(SHARE):
            share_copies[d, s] = remote(
                token_block.at[d, :, mine],
                token_block.at[d, :, mine],
                share_send.at[d, s],
                share_recv.at[d, s],
                heads=flip(head, mask),
            )
            share_copies[d, s].start()

    forward(1)
    forward(2)
    for d in others:
        for s in range(len(SHARE)):
            share_copies[d, s].wait_recv()
        if d == 1:
            forward(3)
        partial_out[d] = jnp.dot(token_block[d], w_query[...], preferred_element_type=f32).astype(
            bf16
        )
        partial_copies[d] = remote(
            partial_out.at[d],
            partial_in.at[d],
            partial_send.at[d],
            partial_recv.at[d],
            batch=flip(plane, d),
        )
        partial_copies[d].start()
        if d == 1:
            send_keys()

    for d in others:
        segment_copies[d].wait_recv()
    count = segment_all.shape[0]
    row_at = lax.broadcasted_iota(jnp.int32, (rows, rows), 0)
    column_at = lax.broadcasted_iota(jnp.int32, (rows, rows), 1)
    own = segment_all[plane, 0:1, 0:rows]
    row_segment = jnp.sum(
        jnp.where(row_at == column_at, jnp.broadcast_to(own, (rows, rows)), 0),
        axis=1,
        keepdims=True,
    )
    segment_row = jnp.concatenate([segment_all[p, 0:1, 0:rows] for p in range(count)], axis=1)
    places = lax.broadcasted_iota(jnp.int32, (rows, count * rows), 1)
    row_places = lax.broadcasted_iota(jnp.int32, (rows, count * rows), 0) + plane * rows
    keep = (segment_row == row_segment) & (places <= row_places)

    for d in others:
        key_copies[d].wait_recv()
        value_copies[d].wait_recv()
    key_block = jnp.concatenate([key_all[p] for p in range(count)], axis=0)
    value_block = jnp.concatenate([value_all[p] for p in range(count)], axis=0)
    for d in others:
        partial_copies[d].wait_recv()
        query = query + partial_in[d].astype(f32)
    query = query.astype(bf16)
    factor = 1.0 / (head_size**0.5)
    attended = []
    for i in range(local_heads):
        scores = (
            lax.dot_general(
                query[:, i * head_size : (i + 1) * head_size],
                key_block,
                (((1,), (1,)), ((), ())),
                preferred_element_type=f32,
            )
            * factor
        )
        top = jnp.max(jnp.where(keep, scores, -1e30), axis=1, keepdims=True)
        weights = jnp.where(keep, jnp.exp(scores - top), 0.0)
        total = jnp.sum(weights, axis=1, keepdims=True)
        gathered = jnp.dot(weights.astype(bf16), value_block, preferred_element_type=f32)
        attended.append((gathered / total).astype(bf16))
    attended_all[plane] = jnp.concatenate(attended, axis=1)

    for d in (2, 3, 1):
        attended_copies[d] = remote(
            attended_all.at[plane],
            attended_all.at[plane],
            attended_send.at[d],
            attended_recv.at[d],
            batch=flip(plane, d),
        )
        attended_copies[d].start()
    for load in out_loads:
        load.wait()
    for d in others:
        attended_copies[d].wait_recv()

    def product(target):
        return lax.dot_general(
            attended_all[target],
            w_out[...],
            (((1,), (1,)), ((), ())),
            preferred_element_type=f32,
        )

    for slot, mask in ((1, 3), (0, 1)):
        core_out[slot] = product(flip(head, mask)).astype(bf16)
        core_copies[slot] = remote(
            core_out.at[slot],
            core_in.at[slot],
            core_send.at[slot],
            core_recv.at[slot],
            heads=flip(head, 1),
        )
        core_copies[slot].start()
    far = product(flip(head, 2))
    core_copies[1].wait_recv()
    chip_out[...] = (far + core_in[1].astype(f32)).astype(bf16)
    chip_copy = remote(chip_out, chip_in, chip_send, chip_recv, heads=flip(head, 2))
    chip_copy.start()
    near = product(head)
    core_copies[0].wait_recv()
    near = near + core_in[0].astype(f32)
    chip_copy.wait_recv()
    final[...] = (near + chip_in[...].astype(f32)).astype(bf16)

    @pl.when(plane != head)
    def _():
        final_copy = remote(final, out, final_send, final_recv, batch=head, heads=plane)
        final_copy.start()
        final_copy.wait()

    @pl.when(plane == head)
    def _():
        final_copy = pltpu.make_async_copy(final, out, final_send)
        final_copy.start()
        final_copy.wait()

    drain()
    chip_copy.wait_send()


SHARE = (1,)


def move_activations(tokens, query_weight, keys, values, segment_ids, out_weight):
    rows, model = tokens.shape
    local_heads, depth, head_size = query_weight.shape
    wide = local_heads * head_size
    count = model // depth
    bf16, dma = jnp.bfloat16, pltpu.SemaphoreType.DMA
    anywhere = pl.BlockSpec(memory_space=pltpu.HBM)
    scratch = [
        pltpu.VMEM((depth, wide), bf16),
        pltpu.VMEM((depth, wide), bf16),
        pltpu.VMEM((count, rows, depth), bf16),
        pltpu.VMEM((count, rows, wide), bf16),
        pltpu.VMEM((count, rows, wide), bf16),
        pltpu.VMEM((count, rows, head_size), bf16),
        pltpu.VMEM((count, rows, head_size), bf16),
        pltpu.VMEM((count, 8, 128), jnp.int32),
        pltpu.VMEM((count, rows, wide), bf16),
        pltpu.VMEM((2, rows, depth), bf16),
        pltpu.VMEM((2, rows, depth), bf16),
        pltpu.VMEM((rows, depth), bf16),
        pltpu.VMEM((rows, depth), bf16),
        pltpu.VMEM((rows, depth), bf16),
        dma((3 + 2 * local_heads,)),
        dma((count,)),
        dma((count,)),
        dma((count, len(SHARE))),
        dma((count, len(SHARE))),
        *[dma((count,)) for _ in range(10)],
        dma((2,)),
        dma((2,)),
        *[dma for _ in range(4)],
    ]
    return pl.pallas_call(
        kernel,
        out_shape=jax.ShapeDtypeStruct((rows, depth), bf16),
        in_specs=[
            anywhere,
            anywhere,
            anywhere,
            anywhere,
            pl.BlockSpec(memory_space=pltpu.VMEM),
            anywhere,
        ],
        out_specs=anywhere,
        scratch_shapes=scratch,
        compiler_params=pltpu.CompilerParams(
            collective_id=0, has_side_effects=True, vmem_limit_bytes=60 * 1024 * 1024
        ),
        cost_estimate=pl.CostEstimate(
            flops=4 * count * rows * depth * wide + 4 * local_heads * count * rows * rows * head_size,
            bytes_accessed=4 * depth * wide + 4 * rows * model,
            transcendentals=local_heads * count * rows * rows,
        ),
    )(tokens, query_weight, keys, values, segment_ids[None, :], out_weight)


def gather_weights(tokens, query_weight, keys, values, segment_ids, out_weight):
    rows = tokens.shape[0]
    head_size = query_weight.shape[2]
    local_heads = query_weight.shape[0]
    kv_local = keys.shape[0]
    sharing = local_heads // kv_local
    first = lax.axis_index("batch") * rows
    places = first + jnp.arange(rows, dtype=jnp.int32)
    query_places = jnp.tile(places, sharing)
    query_segments = jnp.tile(segment_ids, sharing)
    query = jnp.einsum(
        "tc,hcd->htd",
        tokens,
        lax.all_gather(query_weight, "batch", axis=1, tiled=True),
        preferred_element_type=jnp.float32,
    ).astype(jnp.bfloat16)
    query = query.reshape(kv_local, sharing * rows, head_size)
    factor = 1.0 / jnp.sqrt(jnp.float32(head_size))
    begin = (
        jnp.full((kv_local, sharing * rows), -1e30, jnp.float32),
        jnp.zeros((kv_local, sharing * rows), jnp.float32),
        jnp.zeros((kv_local, sharing * rows, head_size), jnp.float32),
    )
    key_piece = lax.all_gather(keys, "batch", axis=1, tiled=True)
    value_piece = lax.all_gather(values, "batch", axis=1, tiled=True)
    segment_piece = lax.all_gather(segment_ids[None, :], "batch", axis=1, tiled=True)
    count = key_piece.shape[1]
    width = 4
    block = width * rows

    def inner(state, number):
        running, total, gathered = state
        offset = number * block
        key_block = lax.dynamic_slice_in_dim(key_piece, offset, block, 1)
        value_block = lax.dynamic_slice_in_dim(value_piece, offset, block, 1)
        segment_block = lax.dynamic_slice_in_dim(segment_piece[0], offset, block, 0)
        scores = (
            jnp.einsum("gqd,gkd->gqk", query, key_block, preferred_element_type=jnp.float32)
            * factor
        )
        key_places = offset + jnp.arange(block, dtype=jnp.int32)
        keep = (segment_block[None, :] == query_segments[:, None]) & (
            key_places[None, :] <= query_places[:, None]
        )
        block_top = jnp.max(jnp.where(keep[None], scores, jnp.float32(-1e30)), axis=2)
        newer = jnp.maximum(running, block_top)
        weights = jnp.where(keep[None], jnp.exp(scores - newer[:, :, None]), jnp.float32(0.0))
        shrink = jnp.exp(running - newer)
        total = total * shrink + jnp.sum(weights, axis=2)
        gathered = gathered * shrink[:, :, None] + jnp.einsum(
            "gqk,gkd->gqd",
            weights,
            value_block.astype(jnp.float32),
            precision=lax.Precision.HIGHEST,
        )
        return ((newer, total, gathered), None)

    result, unused = lax.scan(inner, begin, jnp.arange(count // block, dtype=jnp.int32))
    running, total, gathered = result
    attended = (
        (gathered / total[:, :, None]).astype(jnp.bfloat16).reshape(local_heads, rows, head_size)
    )
    terms = jnp.einsum(
        "htd,hcd->tc",
        attended,
        lax.all_gather(out_weight, "batch", axis=1, tiled=True),
        preferred_element_type=jnp.float32,
    )
    return lax.psum_scatter(terms, "heads", scatter_dimension=1, tiled=True).astype(jnp.bfloat16)


def solution(mesh):
    batch, heads = mesh.shape["batch"], mesh.shape["heads"]

    def on_device(tokens, query_weight, keys, values, segment_ids, out_weight):
        rows, model = tokens.shape
        local_heads, depth, head_size = query_weight.shape
        wide = local_heads * head_size
        weights = 2 * model * wide
        activations = batch * rows * (depth + 3 * wide + depth)
        plan = move_activations if batch == heads == 4 and activations < weights else gather_weights
        return plan(tokens, query_weight, keys, values, segment_ids, out_weight)

    return jax.shard_map(
        on_device,
        mesh=mesh,
        in_specs=(
            P(("groups", "batch"), None),
            P("heads", "batch", None),
            P("heads", ("groups", "batch"), None),
            P("heads", ("groups", "batch"), None),
            P(("groups", "batch")),
            P("heads", "batch", None),
        ),
        out_specs=P(("groups", "batch"), "heads"),
        check_vma=False,
    )
```

```python
import functools

import jax
import jax.numpy as jnp
from jax import lax
from jax.experimental import pallas as pl
from jax.experimental.pallas import tpu as pltpu
from jax.sharding import PartitionSpec as P

MESH = pl.DeviceIdType.MESH


def flip(index, mask):
    bit = 1
    while bit <= mask:
        if mask & bit:
            index = index + bit - 2 * bit * lax.rem(lax.div(index, bit), 2)
        bit *= 2
    return index


def kernel(
    tokens,
    query_weight,
    keys,
    values,
    segments,
    out_weight,
    out,
    w_query,
    w_out,
    token_block,
    partial_out,
    partial_in,
    key_all,
    value_all,
    segment_all,
    attended_all,
    core_out,
    core_in,
    chip_out,
    chip_in,
    final,
    load_sem,
    token_send,
    token_recv,
    share_send,
    share_recv,
    key_send,
    key_recv,
    value_send,
    value_recv,
    segment_send,
    segment_recv,
    partial_send,
    partial_recv,
    attended_send,
    attended_recv,
    core_send,
    core_recv,
    chip_send,
    chip_recv,
    final_send,
    final_recv,
):
    rows, model = tokens.shape
    local_heads, depth, head_size = query_weight.shape
    wide = local_heads * head_size
    plane = lax.axis_index("batch")
    head = lax.axis_index("heads")
    others = (1, 2, 3)
    bf16, f32 = jnp.bfloat16, jnp.float32

    def remote(src, dst, send, recv, **device):
        return pltpu.make_async_remote_copy(
            src_ref=src,
            dst_ref=dst,
            send_sem=send,
            recv_sem=recv,
            device_id=device,
            device_id_type=MESH,
        )

    own_tokens = pltpu.make_async_copy(
        tokens.at[:, pl.ds(pl.multiple_of(plane * depth, depth), depth)],
        token_block.at[0],
        load_sem.at[0],
    )
    own_keys = pltpu.make_async_copy(keys.at[0], key_all.at[plane], load_sem.at[1])
    own_values = pltpu.make_async_copy(values.at[0], value_all.at[plane], load_sem.at[2])
    query_loads = [
        pltpu.make_async_copy(
            query_weight.at[i], w_query.at[:, pl.ds(i * head_size, head_size)], load_sem.at[3 + i]
        )
        for i in range(local_heads)
    ]
    out_loads = [
        pltpu.make_async_copy(
            out_weight.at[i],
            w_out.at[:, pl.ds(i * head_size, head_size)],
            load_sem.at[3 + local_heads + i],
        )
        for i in range(local_heads)
    ]
    for load in [*query_loads, own_tokens, own_keys, own_values, *out_loads]:
        load.start()
    segment_all[plane] = jnp.zeros(segment_all.shape[1:], jnp.int32)
    segment_all[plane, 0:1, 0:rows] = segments[...]

    barrier = pltpu.get_barrier_semaphore()
    for d in others:
        pl.semaphore_signal(
            barrier, inc=1, device_id={"batch": flip(plane, d)}, device_id_type=MESH
        )
        pl.semaphore_signal(barrier, inc=1, device_id={"heads": flip(head, d)}, device_id_type=MESH)

    target, origin = rows_of(head), rows_of(plane)
    stays = (plane == head) & (target == head)

    @pl.when(jnp.logical_not(stays))
    def _():
        pl.semaphore_signal(
            barrier, inc=1, device_id={"batch": head, "heads": origin}, device_id_type=MESH
        )
        pl.semaphore_wait(barrier, 2 * len(others) + 1)

    @pl.when(stays)
    def _():
        pl.semaphore_wait(barrier, 2 * len(others))

    share = depth // (1 + len(SHARE))
    my_share = lax.rem(head, 1 + len(SHARE))
    token_copies, share_copies, key_copies, value_copies, segment_copies = {}, {}, {}, {}, {}
    partial_copies, attended_copies, core_copies, chip_copies = {}, {}, {}, {}

    def drain():
        for copies in (
            token_copies,
            share_copies,
            key_copies,
            value_copies,
            segment_copies,
            partial_copies,
            attended_copies,
            core_copies,
            chip_copies,
        ):
            for copy in copies.values():
                copy.wait_send()

    mine = pl.ds(pl.multiple_of(my_share * share, share), share)
    for d in (2, 3, 1):
        peer = flip(plane, d)
        token_copies[d] = remote(
            tokens.at[:, pl.ds(pl.multiple_of(peer * depth + my_share * share, share), share)],
            token_block.at[d, :, mine],
            token_send.at[d],
            token_recv.at[d],
            batch=peer,
        )
        token_copies[d].start()

    own_keys.wait()
    own_values.wait()

    def send_keys():
        for d in others:
            peer = flip(plane, d)
            key_copies[d] = remote(
                key_all.at[plane], key_all.at[plane], key_send.at[d], key_recv.at[d], batch=peer
            )
            value_copies[d] = remote(
                value_all.at[plane],
                value_all.at[plane],
                value_send.at[d],
                value_recv.at[d],
                batch=peer,
            )
            segment_copies[d] = remote(
                segment_all.at[plane],
                segment_all.at[plane],
                segment_send.at[d],
                segment_recv.at[d],
                batch=peer,
            )
            for copy in (key_copies[d], value_copies[d], segment_copies[d]):
                copy.start()

    send_keys()
    for load in query_loads:
        load.wait()
    own_tokens.wait()
    query = jnp.dot(token_block[0], w_query[...], preferred_element_type=f32)

    def forward(d):
        token_copies[d].wait_recv()
        for s, mask in enumerate(SHARE):
            share_copies[d, s] = remote(
                token_block.at[d, :, mine],
                token_block.at[d, :, mine],
                share_send.at[d, s],
                share_recv.at[d, s],
                heads=flip(head, mask),
            )
            share_copies[d, s].start()

    forward(1)
    forward(2)
    for d in others:
        for s in range(len(SHARE)):
            share_copies[d, s].wait_recv()
        if d == 1:
            forward(3)
        partial_out[d] = jnp.dot(token_block[d], w_query[...], preferred_element_type=f32).astype(
            bf16
        )
        partial_copies[d] = remote(
            partial_out.at[d],
            partial_in.at[d],
            partial_send.at[d],
            partial_recv.at[d],
            batch=flip(plane, d),
        )
        partial_copies[d].start()

    for d in others:
        segment_copies[d].wait_recv()
    count = segment_all.shape[0]
    row_at = lax.broadcasted_iota(jnp.int32, (rows, rows), 0)
    column_at = lax.broadcasted_iota(jnp.int32, (rows, rows), 1)
    own = segment_all[plane, 0:1, 0:rows]
    row_segment = jnp.sum(
        jnp.where(row_at == column_at, jnp.broadcast_to(own, (rows, rows)), 0),
        axis=1,
        keepdims=True,
    )
    segment_row = jnp.concatenate([segment_all[p, 0:1, 0:rows] for p in range(count)], axis=1)
    places = lax.broadcasted_iota(jnp.int32, (rows, count * rows), 1)
    row_places = lax.broadcasted_iota(jnp.int32, (rows, count * rows), 0) + plane * rows
    keep = (segment_row == row_segment) & (places <= row_places)

    for d in others:
        key_copies[d].wait_recv()
        value_copies[d].wait_recv()
    key_block = jnp.concatenate([key_all[p] for p in range(count)], axis=0)
    value_block = jnp.concatenate([value_all[p] for p in range(count)], axis=0)
    for d in others:
        partial_copies[d].wait_recv()
        query = query + partial_in[d].astype(f32)
    query = query.astype(bf16)
    factor = 1.0 / (head_size**0.5)
    attended = []
    for i in range(local_heads):
        scores = (
            lax.dot_general(
                query[:, i * head_size : (i + 1) * head_size],
                key_block,
                (((1,), (1,)), ((), ())),
                preferred_element_type=f32,
            )
            * factor
        )
        top = jnp.max(jnp.where(keep, scores, -1e30), axis=1, keepdims=True)
        weights = jnp.where(keep, jnp.exp(scores - top), 0.0)
        total = jnp.sum(weights, axis=1, keepdims=True)
        gathered = jnp.dot(weights.astype(bf16), value_block, preferred_element_type=f32)
        attended.append((gathered / total).astype(bf16))
    attended_all[plane] = jnp.concatenate(attended, axis=1)

    for d in (2, 3, 1):
        attended_copies[d] = remote(
            attended_all.at[plane],
            attended_all.at[plane],
            attended_send.at[d],
            attended_recv.at[d],
            batch=flip(plane, d),
        )
        attended_copies[d].start()
    for load in out_loads:
        load.wait()
    for d in others:
        attended_copies[d].wait_recv()

    def product(target):
        return lax.dot_general(
            attended_all[target],
            w_out[...],
            (((1,), (1,)), ((), ())),
            preferred_element_type=f32,
        )

    for slot, mask in ((1, 3), (0, 1)):
        core_out[slot] = product(rows_of(flip(head, mask))).astype(bf16)
        core_copies[slot] = remote(
            core_out.at[slot],
            core_in.at[slot],
            core_send.at[slot],
            core_recv.at[slot],
            heads=flip(head, 1),
        )
        core_copies[slot].start()
    far = product(rows_of(flip(head, 2)))
    width = depth // PIECES
    parts = [pl.ds(p * width, width) for p in range(PIECES)]
    core_copies[1].wait_recv()
    for p, part in enumerate(parts):
        chip_out[p] = (far[:, p * width : (p + 1) * width] + core_in[1, :, part].astype(f32)).astype(
            bf16
        )
        chip_copies[p] = remote(
            chip_out.at[p],
            chip_in.at[p],
            chip_send.at[p],
            chip_recv.at[p],
            heads=flip(head, 2),
        )
        chip_copies[p].start()
    near = product(target)
    core_copies[0].wait_recv()
    near = near + core_in[0].astype(f32)
    for p, part in enumerate(parts):
        chip_copies[p].wait_recv()
        final[p] = (near[:, p * width : (p + 1) * width] + chip_in[p].astype(f32)).astype(bf16)
        send = (final.at[p], out.at[:, part], final_send.at[p])

        @pl.when(jnp.logical_not(stays))
        def _():
            remote(*send, final_recv.at[p], batch=target, heads=plane).start()

        @pl.when(stays)
        def _():
            pltpu.make_async_copy(*send).start()

    for p, part in enumerate(parts):
        send = (final.at[p], out.at[:, part], final_send.at[p])

        @pl.when(jnp.logical_not(stays))
        def _():
            remote(*send, final_recv.at[p], batch=target, heads=plane).wait()

        @pl.when(stays)
        def _():
            pltpu.make_async_copy(*send).wait()

    drain()


SHARE = (1, 2, 3)
PIECES = 4


def rows_of(index):
    return 2 * lax.rem(index, 2) + lax.div(index, 2)


def move_activations(tokens, query_weight, keys, values, segment_ids, out_weight):
    rows, model = tokens.shape
    local_heads, depth, head_size = query_weight.shape
    wide = local_heads * head_size
    count = model // depth
    bf16, dma = jnp.bfloat16, pltpu.SemaphoreType.DMA
    anywhere = pl.BlockSpec(memory_space=pltpu.HBM)
    scratch = [
        pltpu.VMEM((depth, wide), bf16),
        pltpu.VMEM((depth, wide), bf16),
        pltpu.VMEM((count, rows, depth), bf16),
        pltpu.VMEM((count, rows, wide), bf16),
        pltpu.VMEM((count, rows, wide), bf16),
        pltpu.VMEM((count, rows, head_size), bf16),
        pltpu.VMEM((count, rows, head_size), bf16),
        pltpu.VMEM((count, 8, 128), jnp.int32),
        pltpu.VMEM((count, rows, wide), bf16),
        pltpu.VMEM((2, rows, depth), bf16),
        pltpu.VMEM((2, rows, depth), bf16),
        pltpu.VMEM((PIECES, rows, depth // PIECES), bf16),
        pltpu.VMEM((PIECES, rows, depth // PIECES), bf16),
        pltpu.VMEM((PIECES, rows, depth // PIECES), bf16),
        dma((3 + 2 * local_heads,)),
        dma((count,)),
        dma((count,)),
        dma((count, len(SHARE))),
        dma((count, len(SHARE))),
        *[dma((count,)) for _ in range(10)],
        dma((2,)),
        dma((2,)),
        *[dma((PIECES,)) for _ in range(4)],
    ]
    return pl.pallas_call(
        kernel,
        out_shape=jax.ShapeDtypeStruct((rows, depth), bf16),
        in_specs=[
            anywhere,
            anywhere,
            anywhere,
            anywhere,
            pl.BlockSpec(memory_space=pltpu.VMEM),
            anywhere,
        ],
        out_specs=anywhere,
        scratch_shapes=scratch,
        compiler_params=pltpu.CompilerParams(
            collective_id=0, has_side_effects=True, vmem_limit_bytes=60 * 1024 * 1024
        ),
        cost_estimate=pl.CostEstimate(
            flops=4 * count * rows * depth * wide + 4 * local_heads * count * rows * rows * head_size,
            bytes_accessed=4 * depth * wide + 4 * rows * model,
            transcendentals=local_heads * count * rows * rows,
        ),
    )(tokens, query_weight, keys, values, segment_ids[None, :], out_weight)


def gather_weights(tokens, query_weight, keys, values, segment_ids, out_weight):
    rows = tokens.shape[0]
    head_size = query_weight.shape[2]
    local_heads = query_weight.shape[0]
    kv_local = keys.shape[0]
    sharing = local_heads // kv_local
    first = lax.axis_index("batch") * rows
    places = first + jnp.arange(rows, dtype=jnp.int32)
    query_places = jnp.tile(places, sharing)
    query_segments = jnp.tile(segment_ids, sharing)
    query = jnp.einsum(
        "tc,hcd->htd",
        tokens,
        lax.all_gather(query_weight, "batch", axis=1, tiled=True),
        preferred_element_type=jnp.float32,
    ).astype(jnp.bfloat16)
    query = query.reshape(kv_local, sharing * rows, head_size)
    factor = 1.0 / jnp.sqrt(jnp.float32(head_size))
    begin = (
        jnp.full((kv_local, sharing * rows), -1e30, jnp.float32),
        jnp.zeros((kv_local, sharing * rows), jnp.float32),
        jnp.zeros((kv_local, sharing * rows, head_size), jnp.float32),
    )
    key_piece = lax.all_gather(keys, "batch", axis=1, tiled=True)
    value_piece = lax.all_gather(values, "batch", axis=1, tiled=True)
    segment_piece = lax.all_gather(segment_ids[None, :], "batch", axis=1, tiled=True)
    count = key_piece.shape[1]
    width = 4
    block = width * rows

    def inner(state, number):
        running, total, gathered = state
        offset = number * block
        key_block = lax.dynamic_slice_in_dim(key_piece, offset, block, 1)
        value_block = lax.dynamic_slice_in_dim(value_piece, offset, block, 1)
        segment_block = lax.dynamic_slice_in_dim(segment_piece[0], offset, block, 0)
        scores = (
            jnp.einsum("gqd,gkd->gqk", query, key_block, preferred_element_type=jnp.float32)
            * factor
        )
        key_places = offset + jnp.arange(block, dtype=jnp.int32)
        keep = (segment_block[None, :] == query_segments[:, None]) & (
            key_places[None, :] <= query_places[:, None]
        )
        block_top = jnp.max(jnp.where(keep[None], scores, jnp.float32(-1e30)), axis=2)
        newer = jnp.maximum(running, block_top)
        weights = jnp.where(keep[None], jnp.exp(scores - newer[:, :, None]), jnp.float32(0.0))
        shrink = jnp.exp(running - newer)
        total = total * shrink + jnp.sum(weights, axis=2)
        gathered = gathered * shrink[:, :, None] + jnp.einsum(
            "gqk,gkd->gqd",
            weights,
            value_block.astype(jnp.float32),
            precision=lax.Precision.HIGHEST,
        )
        return ((newer, total, gathered), None)

    result, unused = lax.scan(inner, begin, jnp.arange(count // block, dtype=jnp.int32))
    running, total, gathered = result
    attended = (
        (gathered / total[:, :, None]).astype(jnp.bfloat16).reshape(local_heads, rows, head_size)
    )
    terms = jnp.einsum(
        "htd,hcd->tc",
        attended,
        lax.all_gather(out_weight, "batch", axis=1, tiled=True),
        preferred_element_type=jnp.float32,
    )
    return lax.psum_scatter(terms, "heads", scatter_dimension=1, tiled=True).astype(jnp.bfloat16)


def solution(mesh):
    batch, heads = mesh.shape["batch"], mesh.shape["heads"]

    def on_device(tokens, query_weight, keys, values, segment_ids, out_weight):
        rows, model = tokens.shape
        local_heads, depth, head_size = query_weight.shape
        wide = local_heads * head_size
        weights = 2 * model * wide
        activations = batch * rows * (depth + 3 * wide + depth)
        plan = move_activations if batch == heads == 4 and activations < weights else gather_weights
        return plan(tokens, query_weight, keys, values, segment_ids, out_weight)

    return jax.shard_map(
        on_device,
        mesh=mesh,
        in_specs=(
            P(("groups", "batch"), None),
            P("heads", "batch", None),
            P("heads", ("groups", "batch"), None),
            P("heads", ("groups", "batch"), None),
            P(("groups", "batch")),
            P("heads", "batch", None),
        ),
        out_specs=P(("groups", "batch"), "heads"),
        check_vma=False,
    )
```

```python
import functools

import jax
import jax.numpy as jnp
from jax import lax
from jax.experimental import pallas as pl
from jax.experimental.pallas import tpu as pltpu
from jax.sharding import PartitionSpec as P

MESH = pl.DeviceIdType.MESH


def flip(index, mask):
    bit = 1
    while bit <= mask:
        if mask & bit:
            index = index + bit - 2 * bit * lax.rem(lax.div(index, bit), 2)
        bit *= 2
    return index


def kernel(
    tokens,
    query_weight,
    keys,
    values,
    segments,
    out_weight,
    out,
    w_query,
    w_out,
    token_block,
    partial_out,
    partial_in,
    key_all,
    value_all,
    segment_all,
    attended_all,
    core_out,
    core_in,
    chip_out,
    chip_in,
    final,
    kept,
    load_sem,
    token_send,
    token_recv,
    share_send,
    share_recv,
    key_send,
    key_recv,
    value_send,
    value_recv,
    segment_send,
    segment_recv,
    partial_send,
    partial_recv,
    attended_send,
    attended_recv,
    core_send,
    core_recv,
    chip_send,
    chip_recv,
    final_send,
    final_recv,
):
    rows, model = tokens.shape
    local_heads, depth, head_size = query_weight.shape
    wide = local_heads * head_size
    plane = lax.axis_index("batch")
    head = lax.axis_index("heads")
    others = (1, 2, 3)
    head_columns = [pl.ds(i * head_size, head_size) for i in range(local_heads)]
    bf16, f32 = jnp.bfloat16, jnp.float32

    def remote(src, dst, send, recv, **device):
        return pltpu.make_async_remote_copy(
            src_ref=src,
            dst_ref=dst,
            send_sem=send,
            recv_sem=recv,
            device_id=device,
            device_id_type=MESH,
        )

    own_tokens = pltpu.make_async_copy(
        tokens.at[:, pl.ds(pl.multiple_of(plane * depth, depth), depth)],
        token_block.at[0],
        load_sem.at[0],
    )
    own_keys = pltpu.make_async_copy(keys.at[0], key_all.at[plane], load_sem.at[1])
    own_values = pltpu.make_async_copy(values.at[0], value_all.at[plane], load_sem.at[2])
    query_loads = [
        pltpu.make_async_copy(
            query_weight.at[i], w_query.at[:, pl.ds(i * head_size, head_size)], load_sem.at[3 + i]
        )
        for i in range(local_heads)
    ]
    out_loads = [
        pltpu.make_async_copy(
            out_weight.at[i],
            w_out.at[:, pl.ds(i * head_size, head_size)],
            load_sem.at[3 + local_heads + i],
        )
        for i in range(local_heads)
    ]
    for load in [*query_loads, own_tokens, own_keys, own_values, *out_loads]:
        load.start()
    segment_all[plane] = jnp.zeros(segment_all.shape[1:], jnp.int32)
    segment_all[plane, 0:1, 0:rows] = segments[...]

    barrier = pltpu.get_barrier_semaphore()
    for d in others:
        pl.semaphore_signal(
            barrier, inc=1, device_id={"batch": flip(plane, d)}, device_id_type=MESH
        )
        pl.semaphore_signal(barrier, inc=1, device_id={"heads": flip(head, d)}, device_id_type=MESH)

    target, origin = rows_of(head), rows_of(plane)
    stays = (plane == head) & (target == head)

    @pl.when(jnp.logical_not(stays))
    def _():
        pl.semaphore_signal(
            barrier, inc=1, device_id={"batch": head, "heads": origin}, device_id_type=MESH
        )
        pl.semaphore_wait(barrier, 2 * len(others) + 1)

    @pl.when(stays)
    def _():
        pl.semaphore_wait(barrier, 2 * len(others))

    share = depth // (1 + len(SHARE))
    my_share = lax.rem(head, 1 + len(SHARE))
    token_copies, share_copies, key_copies, value_copies, segment_copies = {}, {}, {}, {}, {}
    partial_copies, attended_copies, core_copies, chip_copies = {}, {}, {}, {}

    def drain():
        for copies in (
            token_copies,
            share_copies,
            key_copies,
            value_copies,
            segment_copies,
            partial_copies,
            attended_copies,
            core_copies,
            chip_copies,
        ):
            for copy in copies.values():
                copy.wait_send()

    mine = pl.ds(pl.multiple_of(my_share * share, share), share)
    for d in (2, 3, 1):
        peer = flip(plane, d)
        token_copies[d] = remote(
            tokens.at[:, pl.ds(pl.multiple_of(peer * depth + my_share * share, share), share)],
            token_block.at[d, :, mine],
            token_send.at[d],
            token_recv.at[d],
            batch=peer,
        )
        token_copies[d].start()

    own_keys.wait()
    own_values.wait()

    def send_keys():
        for d in others:
            peer = flip(plane, d)
            key_copies[d] = remote(
                key_all.at[plane], key_all.at[plane], key_send.at[d], key_recv.at[d], batch=peer
            )
            value_copies[d] = remote(
                value_all.at[plane],
                value_all.at[plane],
                value_send.at[d],
                value_recv.at[d],
                batch=peer,
            )
            segment_copies[d] = remote(
                segment_all.at[plane],
                segment_all.at[plane],
                segment_send.at[d],
                segment_recv.at[d],
                batch=peer,
            )
            for copy in (key_copies[d], value_copies[d], segment_copies[d]):
                copy.start()

    send_keys()
    for load in query_loads:
        load.wait()
    own_tokens.wait()
    query = jnp.dot(token_block[0], w_query[...], preferred_element_type=f32)

    def forward(d):
        token_copies[d].wait_recv()
        for s, mask in enumerate(SHARE):
            share_copies[d, s] = remote(
                token_block.at[d, :, mine],
                token_block.at[d, :, mine],
                share_send.at[d, s],
                share_recv.at[d, s],
                heads=flip(head, mask),
            )
            share_copies[d, s].start()

    forward(1)
    forward(2)
    for d in others:
        for s in range(len(SHARE)):
            share_copies[d, s].wait_recv()
        if d == 1:
            forward(3)
        partial_out[d] = jnp.dot(token_block[d], w_query[...], preferred_element_type=f32).astype(
            bf16
        )
        for i, columns in enumerate(head_columns):
            partial_copies[d, i] = remote(
                partial_out.at[d, :, columns],
                partial_in.at[d, :, columns],
                partial_send.at[d, i],
                partial_recv.at[d, i],
                batch=flip(plane, d),
            )
            partial_copies[d, i].start()

    for d in others:
        segment_copies[d].wait_recv()
    count = segment_all.shape[0]
    row_at = lax.broadcasted_iota(jnp.int32, (rows, rows), 0)
    column_at = lax.broadcasted_iota(jnp.int32, (rows, rows), 1)
    own = segment_all[plane, 0:1, 0:rows]
    row_segment = jnp.sum(
        jnp.where(row_at == column_at, jnp.broadcast_to(own, (rows, rows)), 0),
        axis=1,
        keepdims=True,
    )
    segment_row = jnp.concatenate([segment_all[p, 0:1, 0:rows] for p in range(count)], axis=1)
    places = lax.broadcasted_iota(jnp.int32, (rows, count * rows), 1)
    row_places = lax.broadcasted_iota(jnp.int32, (rows, count * rows), 0) + plane * rows
    keep = (segment_row == row_segment) & (places <= row_places)

    for d in others:
        key_copies[d].wait_recv()
        value_copies[d].wait_recv()
    key_block = jnp.concatenate([key_all[p] for p in range(count)], axis=0)
    value_block = jnp.concatenate([value_all[p] for p in range(count)], axis=0)
    factor = 1.0 / (head_size**0.5)
    for i, columns in enumerate(head_columns):
        head_query = query[:, i * head_size : (i + 1) * head_size]
        for d in others:
            partial_copies[d, i].wait_recv()
            head_query = head_query + partial_in[d, :, columns].astype(f32)
        scores = (
            lax.dot_general(
                head_query.astype(bf16),
                key_block,
                (((1,), (1,)), ((), ())),
                preferred_element_type=f32,
            )
            * factor
        )
        top = jnp.max(jnp.where(keep, scores, -1e30), axis=1, keepdims=True)
        weights = jnp.where(keep, jnp.exp(scores - top), 0.0)
        total = jnp.sum(weights, axis=1, keepdims=True)
        gathered = jnp.dot(weights.astype(bf16), value_block, preferred_element_type=f32)
        attended_all[plane, :, columns] = (gathered / total).astype(bf16)
        for d in (2, 3, 1):
            attended_copies[d, i] = remote(
                attended_all.at[plane, :, columns],
                attended_all.at[plane, :, columns],
                attended_send.at[d, i],
                attended_recv.at[d, i],
                batch=flip(plane, d),
            )
            attended_copies[d, i].start()
    for load in out_loads:
        load.wait()

    def product(target):
        return lax.dot_general(
            attended_all[target],
            w_out[...],
            (((1,), (1,)), ((), ())),
            preferred_element_type=f32,
        )

    for slot in range(2):
        core_copies[slot] = remote(
            core_out.at[slot],
            core_in.at[slot],
            core_send.at[slot],
            core_recv.at[slot],
            heads=flip(head, 1),
        )
    for d in (0, *others):
        if d:
            for i in range(local_heads):
                attended_copies[d, i].wait_recv()
        rows_at = flip(plane, d)
        adder = rows_of(rows_at)
        term = product(rows_at)
        here = lax.rem(adder, 2) == lax.rem(head, 2)
        for slot in range(2):
            same = lax.div(adder, 2) == lax.div(head, 2)
            this = same if slot == 0 else jnp.logical_not(same)

            @pl.when(here & this)
            def _():
                kept[slot] = term

            @pl.when(jnp.logical_not(here) & this)
            def _():
                core_out[slot] = term.astype(bf16)
                core_copies[slot].start()

    width = depth // PIECES
    parts = [pl.ds(p * width, width) for p in range(PIECES)]
    core_copies[1].wait_recv()
    for p, part in enumerate(parts):
        chip_out[p] = (kept[1, :, part] + core_in[1, :, part].astype(f32)).astype(
            bf16
        )
        chip_copies[p] = remote(
            chip_out.at[p],
            chip_in.at[p],
            chip_send.at[p],
            chip_recv.at[p],
            heads=flip(head, 2),
        )
        chip_copies[p].start()
    core_copies[0].wait_recv()
    near = kept[0] + core_in[0].astype(f32)
    for p, part in enumerate(parts):
        chip_copies[p].wait_recv()
        final[p] = (near[:, p * width : (p + 1) * width] + chip_in[p].astype(f32)).astype(bf16)
        send = (final.at[p], out.at[:, part], final_send.at[p])

        @pl.when(jnp.logical_not(stays))
        def _():
            remote(*send, final_recv.at[p], batch=target, heads=plane).start()

        @pl.when(stays)
        def _():
            pltpu.make_async_copy(*send).start()

    for p, part in enumerate(parts):
        send = (final.at[p], out.at[:, part], final_send.at[p])

        @pl.when(jnp.logical_not(stays))
        def _():
            remote(*send, final_recv.at[p], batch=target, heads=plane).wait()

        @pl.when(stays)
        def _():
            pltpu.make_async_copy(*send).wait()

    drain()


SHARE = (1, 2, 3)
PIECES = 4


def rows_of(index):
    return 2 * lax.rem(index, 2) + lax.div(index, 2)


def move_activations(tokens, query_weight, keys, values, segment_ids, out_weight):
    rows, model = tokens.shape
    local_heads, depth, head_size = query_weight.shape
    wide = local_heads * head_size
    count = model // depth
    bf16, dma = jnp.bfloat16, pltpu.SemaphoreType.DMA
    anywhere = pl.BlockSpec(memory_space=pltpu.HBM)
    scratch = [
        pltpu.VMEM((depth, wide), bf16),
        pltpu.VMEM((depth, wide), bf16),
        pltpu.VMEM((count, rows, depth), bf16),
        pltpu.VMEM((count, rows, wide), bf16),
        pltpu.VMEM((count, rows, wide), bf16),
        pltpu.VMEM((count, rows, head_size), bf16),
        pltpu.VMEM((count, rows, head_size), bf16),
        pltpu.VMEM((count, 8, 128), jnp.int32),
        pltpu.VMEM((count, rows, wide), bf16),
        pltpu.VMEM((2, rows, depth), bf16),
        pltpu.VMEM((2, rows, depth), bf16),
        pltpu.VMEM((PIECES, rows, depth // PIECES), bf16),
        pltpu.VMEM((PIECES, rows, depth // PIECES), bf16),
        pltpu.VMEM((PIECES, rows, depth // PIECES), bf16),
        pltpu.VMEM((2, rows, depth), jnp.float32),
        dma((3 + 2 * local_heads,)),
        dma((count,)),
        dma((count,)),
        dma((count, len(SHARE))),
        dma((count, len(SHARE))),
        *[dma((count,)) for _ in range(6)],
        *[dma((count, local_heads)) for _ in range(4)],
        dma((2,)),
        dma((2,)),
        *[dma((PIECES,)) for _ in range(4)],
    ]
    return pl.pallas_call(
        kernel,
        out_shape=jax.ShapeDtypeStruct((rows, depth), bf16),
        in_specs=[
            anywhere,
            anywhere,
            anywhere,
            anywhere,
            pl.BlockSpec(memory_space=pltpu.VMEM),
            anywhere,
        ],
        out_specs=anywhere,
        scratch_shapes=scratch,
        compiler_params=pltpu.CompilerParams(
            collective_id=0, has_side_effects=True, vmem_limit_bytes=60 * 1024 * 1024
        ),
        cost_estimate=pl.CostEstimate(
            flops=4 * count * rows * depth * wide + 4 * local_heads * count * rows * rows * head_size,
            bytes_accessed=4 * depth * wide + 4 * rows * model,
            transcendentals=local_heads * count * rows * rows,
        ),
    )(tokens, query_weight, keys, values, segment_ids[None, :], out_weight)


def gather_weights(tokens, query_weight, keys, values, segment_ids, out_weight):
    rows = tokens.shape[0]
    head_size = query_weight.shape[2]
    local_heads = query_weight.shape[0]
    kv_local = keys.shape[0]
    sharing = local_heads // kv_local
    first = lax.axis_index("batch") * rows
    places = first + jnp.arange(rows, dtype=jnp.int32)
    query_places = jnp.tile(places, sharing)
    query_segments = jnp.tile(segment_ids, sharing)
    query = jnp.einsum(
        "tc,hcd->htd",
        tokens,
        lax.all_gather(query_weight, "batch", axis=1, tiled=True),
        preferred_element_type=jnp.float32,
    ).astype(jnp.bfloat16)
    query = query.reshape(kv_local, sharing * rows, head_size)
    factor = 1.0 / jnp.sqrt(jnp.float32(head_size))
    begin = (
        jnp.full((kv_local, sharing * rows), -1e30, jnp.float32),
        jnp.zeros((kv_local, sharing * rows), jnp.float32),
        jnp.zeros((kv_local, sharing * rows, head_size), jnp.float32),
    )
    key_piece = lax.all_gather(keys, "batch", axis=1, tiled=True)
    value_piece = lax.all_gather(values, "batch", axis=1, tiled=True)
    segment_piece = lax.all_gather(segment_ids[None, :], "batch", axis=1, tiled=True)
    count = key_piece.shape[1]
    width = 4
    block = width * rows

    def inner(state, number):
        running, total, gathered = state
        offset = number * block
        key_block = lax.dynamic_slice_in_dim(key_piece, offset, block, 1)
        value_block = lax.dynamic_slice_in_dim(value_piece, offset, block, 1)
        segment_block = lax.dynamic_slice_in_dim(segment_piece[0], offset, block, 0)
        scores = (
            jnp.einsum("gqd,gkd->gqk", query, key_block, preferred_element_type=jnp.float32)
            * factor
        )
        key_places = offset + jnp.arange(block, dtype=jnp.int32)
        keep = (segment_block[None, :] == query_segments[:, None]) & (
            key_places[None, :] <= query_places[:, None]
        )
        block_top = jnp.max(jnp.where(keep[None], scores, jnp.float32(-1e30)), axis=2)
        newer = jnp.maximum(running, block_top)
        weights = jnp.where(keep[None], jnp.exp(scores - newer[:, :, None]), jnp.float32(0.0))
        shrink = jnp.exp(running - newer)
        total = total * shrink + jnp.sum(weights, axis=2)
        gathered = gathered * shrink[:, :, None] + jnp.einsum(
            "gqk,gkd->gqd",
            weights,
            value_block.astype(jnp.float32),
            precision=lax.Precision.HIGHEST,
        )
        return ((newer, total, gathered), None)

    result, unused = lax.scan(inner, begin, jnp.arange(count // block, dtype=jnp.int32))
    running, total, gathered = result
    attended = (
        (gathered / total[:, :, None]).astype(jnp.bfloat16).reshape(local_heads, rows, head_size)
    )
    terms = jnp.einsum(
        "htd,hcd->tc",
        attended,
        lax.all_gather(out_weight, "batch", axis=1, tiled=True),
        preferred_element_type=jnp.float32,
    )
    return lax.psum_scatter(terms, "heads", scatter_dimension=1, tiled=True).astype(jnp.bfloat16)


def solution(mesh):
    batch, heads = mesh.shape["batch"], mesh.shape["heads"]

    def on_device(tokens, query_weight, keys, values, segment_ids, out_weight):
        rows, model = tokens.shape
        local_heads, depth, head_size = query_weight.shape
        wide = local_heads * head_size
        weights = 2 * model * wide
        activations = batch * rows * (depth + 3 * wide + depth)
        plan = move_activations if batch == heads == 4 and activations < weights else gather_weights
        return plan(tokens, query_weight, keys, values, segment_ids, out_weight)

    return jax.shard_map(
        on_device,
        mesh=mesh,
        in_specs=(
            P(("groups", "batch"), None),
            P("heads", "batch", None),
            P("heads", ("groups", "batch"), None),
            P("heads", ("groups", "batch"), None),
            P(("groups", "batch")),
            P("heads", "batch", None),
        ),
        out_specs=P(("groups", "batch"), "heads"),
        check_vma=False,
    )
```

```python
import functools

import jax
import jax.numpy as jnp
from jax import lax
from jax.experimental import pallas as pl
from jax.experimental.pallas import tpu as pltpu
from jax.sharding import PartitionSpec as P

MESH = pl.DeviceIdType.MESH


def flip(index, mask):
    bit = 1
    while bit <= mask:
        if mask & bit:
            index = index + bit - 2 * bit * lax.rem(lax.div(index, bit), 2)
        bit *= 2
    return index


def kernel(
    tokens,
    query_weight,
    keys,
    values,
    segments,
    out_weight,
    out,
    w_query,
    w_out,
    token_block,
    partial_out,
    partial_in,
    key_all,
    value_all,
    segment_all,
    attended_all,
    core_out,
    core_in,
    chip_out,
    chip_in,
    final,
    kept,
    load_sem,
    token_send,
    token_recv,
    share_send,
    share_recv,
    key_send,
    key_recv,
    value_send,
    value_recv,
    segment_send,
    segment_recv,
    partial_send,
    partial_recv,
    attended_send,
    attended_recv,
    core_send,
    core_recv,
    chip_send,
    chip_recv,
    final_send,
    final_recv,
):
    rows, model = tokens.shape
    local_heads, depth, head_size = query_weight.shape
    wide = local_heads * head_size
    plane = lax.axis_index("batch")
    head = lax.axis_index("heads")
    others = (1, 2, 3)
    head_columns = [pl.ds(i * head_size, head_size) for i in range(local_heads)]
    bf16, f32 = jnp.bfloat16, jnp.float32

    def remote(src, dst, send, recv, **device):
        return pltpu.make_async_remote_copy(
            src_ref=src,
            dst_ref=dst,
            send_sem=send,
            recv_sem=recv,
            device_id=device,
            device_id_type=MESH,
        )

    own_tokens = pltpu.make_async_copy(
        tokens.at[:, pl.ds(pl.multiple_of(plane * depth, depth), depth)],
        token_block.at[0],
        load_sem.at[0],
    )
    own_keys = pltpu.make_async_copy(keys.at[0], key_all.at[plane], load_sem.at[1])
    own_values = pltpu.make_async_copy(values.at[0], value_all.at[plane], load_sem.at[2])
    query_loads = [
        pltpu.make_async_copy(
            query_weight.at[i], w_query.at[:, pl.ds(i * head_size, head_size)], load_sem.at[3 + i]
        )
        for i in range(local_heads)
    ]
    out_loads = [
        pltpu.make_async_copy(
            out_weight.at[i],
            w_out.at[:, pl.ds(i * head_size, head_size)],
            load_sem.at[3 + local_heads + i],
        )
        for i in range(local_heads)
    ]
    for load in [*query_loads, own_tokens, own_keys, own_values, *out_loads]:
        load.start()
    segment_all[plane] = jnp.zeros(segment_all.shape[1:], jnp.int32)
    segment_all[plane, 0:1, 0:rows] = segments[...]

    barrier = pltpu.get_barrier_semaphore()
    for d in others:
        pl.semaphore_signal(
            barrier, inc=1, device_id={"batch": flip(plane, d)}, device_id_type=MESH
        )
        pl.semaphore_signal(barrier, inc=1, device_id={"heads": flip(head, d)}, device_id_type=MESH)

    target, origin = rows_of(head), rows_of(plane)
    stays = (plane == head) & (target == head)

    @pl.when(jnp.logical_not(stays))
    def _():
        pl.semaphore_signal(
            barrier, inc=1, device_id={"batch": head, "heads": origin}, device_id_type=MESH
        )
        pl.semaphore_wait(barrier, 2 * len(others) + 1)

    @pl.when(stays)
    def _():
        pl.semaphore_wait(barrier, 2 * len(others))

    share = depth // (1 + len(SHARE))
    my_share = lax.rem(head, 1 + len(SHARE))
    token_copies, share_copies, key_copies, value_copies, segment_copies = {}, {}, {}, {}, {}
    partial_copies, attended_copies, core_copies, chip_copies = {}, {}, {}, {}

    def drain():
        for copies in (
            token_copies,
            share_copies,
            key_copies,
            value_copies,
            segment_copies,
            partial_copies,
            attended_copies,
            core_copies,
            chip_copies,
        ):
            for copy in copies.values():
                copy.wait_send()

    mine = pl.ds(pl.multiple_of(my_share * share, share), share)
    for d in (2, 3, 1):
        peer = flip(plane, d)
        token_copies[d] = remote(
            tokens.at[:, pl.ds(pl.multiple_of(peer * depth + my_share * share, share), share)],
            token_block.at[d, :, mine],
            token_send.at[d],
            token_recv.at[d],
            batch=peer,
        )
        token_copies[d].start()

    own_keys.wait()
    own_values.wait()

    def send_keys():
        for d in others:
            peer = flip(plane, d)
            key_copies[d] = remote(
                key_all.at[plane], key_all.at[plane], key_send.at[d], key_recv.at[d], batch=peer
            )
            value_copies[d] = remote(
                value_all.at[plane],
                value_all.at[plane],
                value_send.at[d],
                value_recv.at[d],
                batch=peer,
            )
            segment_copies[d] = remote(
                segment_all.at[plane],
                segment_all.at[plane],
                segment_send.at[d],
                segment_recv.at[d],
                batch=peer,
            )
            for copy in (key_copies[d], value_copies[d], segment_copies[d]):
                copy.start()

    send_keys()
    for load in query_loads:
        load.wait()
    own_tokens.wait()

    def forward(d):
        token_copies[d].wait_recv()
        for s, mask in enumerate(SHARE):
            share_copies[d, s] = remote(
                token_block.at[d, :, mine],
                token_block.at[d, :, mine],
                share_send.at[d, s],
                share_recv.at[d, s],
                heads=flip(head, mask),
            )
            share_copies[d, s].start()

    forward(1)
    forward(2)
    query = jnp.dot(token_block[0], w_query[...], preferred_element_type=f32)
    for d in others:
        for s in range(len(SHARE)):
            share_copies[d, s].wait_recv()
        if d == 1:
            forward(3)
        partial_out[d] = jnp.dot(token_block[d], w_query[...], preferred_element_type=f32).astype(
            bf16
        )
        for i, columns in enumerate(head_columns):
            partial_copies[d, i] = remote(
                partial_out.at[d, :, columns],
                partial_in.at[d, :, columns],
                partial_send.at[d, i],
                partial_recv.at[d, i],
                batch=flip(plane, d),
            )
            partial_copies[d, i].start()

    for d in others:
        segment_copies[d].wait_recv()
    count = segment_all.shape[0]
    row_at = lax.broadcasted_iota(jnp.int32, (rows, rows), 0)
    column_at = lax.broadcasted_iota(jnp.int32, (rows, rows), 1)
    own = segment_all[plane, 0:1, 0:rows]
    row_segment = jnp.sum(
        jnp.where(row_at == column_at, jnp.broadcast_to(own, (rows, rows)), 0),
        axis=1,
        keepdims=True,
    )
    segment_row = jnp.concatenate([segment_all[p, 0:1, 0:rows] for p in range(count)], axis=1)
    places = lax.broadcasted_iota(jnp.int32, (rows, count * rows), 1)
    row_places = lax.broadcasted_iota(jnp.int32, (rows, count * rows), 0) + plane * rows
    keep = (segment_row == row_segment) & (places <= row_places)

    for d in others:
        key_copies[d].wait_recv()
        value_copies[d].wait_recv()
    key_block = jnp.concatenate([key_all[p] for p in range(count)], axis=0)
    value_block = jnp.concatenate([value_all[p] for p in range(count)], axis=0)
    factor = 1.0 / (head_size**0.5)
    for i, columns in enumerate(head_columns):
        head_query = query[:, i * head_size : (i + 1) * head_size]
        for d in others:
            partial_copies[d, i].wait_recv()
            head_query = head_query + partial_in[d, :, columns].astype(f32)
        scores = (
            lax.dot_general(
                head_query.astype(bf16),
                key_block,
                (((1,), (1,)), ((), ())),
                preferred_element_type=f32,
            )
            * factor
        )
        top = jnp.max(jnp.where(keep, scores, -1e30), axis=1, keepdims=True)
        weights = jnp.where(keep, jnp.exp(scores - top), 0.0)
        total = jnp.sum(weights, axis=1, keepdims=True)
        gathered = jnp.dot(weights.astype(bf16), value_block, preferred_element_type=f32)
        attended_all[plane, :, columns] = (gathered / total).astype(bf16)
        for d in (2, 3, 1):
            attended_copies[d, i] = remote(
                attended_all.at[plane, :, columns],
                attended_all.at[plane, :, columns],
                attended_send.at[d, i],
                attended_recv.at[d, i],
                batch=flip(plane, d),
            )
            attended_copies[d, i].start()
    for load in out_loads:
        load.wait()

    def product(target):
        return lax.dot_general(
            attended_all[target],
            w_out[...],
            (((1,), (1,)), ((), ())),
            preferred_element_type=f32,
        )

    for slot in range(2):
        core_copies[slot] = remote(
            core_out.at[slot],
            core_in.at[slot],
            core_send.at[slot],
            core_recv.at[slot],
            heads=flip(head, 1),
        )
    width = depth // PIECES
    parts = [pl.ds(p * width, width) for p in range(PIECES)]
    for p in range(PIECES):
        chip_copies[p] = remote(
            chip_out.at[p],
            chip_in.at[p],
            chip_send.at[p],
            chip_recv.at[p],
            heads=flip(head, 2),
        )

    def send_chip(d):
        @pl.when(rows_of(flip(plane, d)) == flip(head, 2))
        def _():
            core_copies[1].wait_recv()
            for p, part in enumerate(parts):
                chip_out[p] = (kept[1, :, part] + core_in[1, :, part].astype(f32)).astype(bf16)
                chip_copies[p].start()

    for d in (0, *others):
        if d:
            for i in range(local_heads):
                attended_copies[d, i].wait_recv()
        rows_at = flip(plane, d)
        adder = rows_of(rows_at)
        term = product(rows_at)
        here = lax.rem(adder, 2) == lax.rem(head, 2)
        for slot in range(2):
            same = lax.div(adder, 2) == lax.div(head, 2)
            this = same if slot == 0 else jnp.logical_not(same)

            @pl.when(here & this)
            def _():
                kept[slot] = term

            @pl.when(jnp.logical_not(here) & this)
            def _():
                core_out[slot] = term.astype(bf16)
                core_copies[slot].start()

        if d:
            send_chip(d - 1)
    send_chip(others[-1])
    core_copies[0].wait_recv()
    near = kept[0] + core_in[0].astype(f32)
    for p, part in enumerate(parts):
        chip_copies[p].wait_recv()
        final[p] = (near[:, p * width : (p + 1) * width] + chip_in[p].astype(f32)).astype(bf16)
        send = (final.at[p], out.at[:, part], final_send.at[p])

        @pl.when(jnp.logical_not(stays))
        def _():
            remote(*send, final_recv.at[p], batch=target, heads=plane).start()

        @pl.when(stays)
        def _():
            pltpu.make_async_copy(*send).start()

    for p, part in enumerate(parts):
        send = (final.at[p], out.at[:, part], final_send.at[p])

        @pl.when(jnp.logical_not(stays))
        def _():
            remote(*send, final_recv.at[p], batch=target, heads=plane).wait()

        @pl.when(stays)
        def _():
            pltpu.make_async_copy(*send).wait()

    drain()


SHARE = (1, 2, 3)
PIECES = 4


def rows_of(index):
    return 2 * lax.rem(index, 2) + lax.div(index, 2)


def move_activations(tokens, query_weight, keys, values, segment_ids, out_weight):
    rows, model = tokens.shape
    local_heads, depth, head_size = query_weight.shape
    wide = local_heads * head_size
    count = model // depth
    bf16, dma = jnp.bfloat16, pltpu.SemaphoreType.DMA
    anywhere = pl.BlockSpec(memory_space=pltpu.HBM)
    scratch = [
        pltpu.VMEM((depth, wide), bf16),
        pltpu.VMEM((depth, wide), bf16),
        pltpu.VMEM((count, rows, depth), bf16),
        pltpu.VMEM((count, rows, wide), bf16),
        pltpu.VMEM((count, rows, wide), bf16),
        pltpu.VMEM((count, rows, head_size), bf16),
        pltpu.VMEM((count, rows, head_size), bf16),
        pltpu.VMEM((count, 8, 128), jnp.int32),
        pltpu.VMEM((count, rows, wide), bf16),
        pltpu.VMEM((2, rows, depth), bf16),
        pltpu.VMEM((2, rows, depth), bf16),
        pltpu.VMEM((PIECES, rows, depth // PIECES), bf16),
        pltpu.VMEM((PIECES, rows, depth // PIECES), bf16),
        pltpu.VMEM((PIECES, rows, depth // PIECES), bf16),
        pltpu.VMEM((2, rows, depth), jnp.float32),
        dma((3 + 2 * local_heads,)),
        dma((count,)),
        dma((count,)),
        dma((count, len(SHARE))),
        dma((count, len(SHARE))),
        *[dma((count,)) for _ in range(6)],
        *[dma((count, local_heads)) for _ in range(4)],
        dma((2,)),
        dma((2,)),
        *[dma((PIECES,)) for _ in range(4)],
    ]
    return pl.pallas_call(
        kernel,
        out_shape=jax.ShapeDtypeStruct((rows, depth), bf16),
        in_specs=[
            anywhere,
            anywhere,
            anywhere,
            anywhere,
            pl.BlockSpec(memory_space=pltpu.VMEM),
            anywhere,
        ],
        out_specs=anywhere,
        scratch_shapes=scratch,
        compiler_params=pltpu.CompilerParams(
            collective_id=0, has_side_effects=True, vmem_limit_bytes=60 * 1024 * 1024
        ),
        cost_estimate=pl.CostEstimate(
            flops=4 * count * rows * depth * wide + 4 * local_heads * count * rows * rows * head_size,
            bytes_accessed=4 * depth * wide + 4 * rows * model,
            transcendentals=local_heads * count * rows * rows,
        ),
    )(tokens, query_weight, keys, values, segment_ids[None, :], out_weight)


def gather_weights(tokens, query_weight, keys, values, segment_ids, out_weight):
    rows = tokens.shape[0]
    head_size = query_weight.shape[2]
    local_heads = query_weight.shape[0]
    kv_local = keys.shape[0]
    sharing = local_heads // kv_local
    first = lax.axis_index("batch") * rows
    places = first + jnp.arange(rows, dtype=jnp.int32)
    query_places = jnp.tile(places, sharing)
    query_segments = jnp.tile(segment_ids, sharing)
    query = jnp.einsum(
        "tc,hcd->htd",
        tokens,
        lax.all_gather(query_weight, "batch", axis=1, tiled=True),
        preferred_element_type=jnp.float32,
    ).astype(jnp.bfloat16)
    query = query.reshape(kv_local, sharing * rows, head_size)
    factor = 1.0 / jnp.sqrt(jnp.float32(head_size))
    begin = (
        jnp.full((kv_local, sharing * rows), -1e30, jnp.float32),
        jnp.zeros((kv_local, sharing * rows), jnp.float32),
        jnp.zeros((kv_local, sharing * rows, head_size), jnp.float32),
    )
    key_piece = lax.all_gather(keys, "batch", axis=1, tiled=True)
    value_piece = lax.all_gather(values, "batch", axis=1, tiled=True)
    segment_piece = lax.all_gather(segment_ids[None, :], "batch", axis=1, tiled=True)
    count = key_piece.shape[1]
    width = 4
    block = width * rows

    def inner(state, number):
        running, total, gathered = state
        offset = number * block
        key_block = lax.dynamic_slice_in_dim(key_piece, offset, block, 1)
        value_block = lax.dynamic_slice_in_dim(value_piece, offset, block, 1)
        segment_block = lax.dynamic_slice_in_dim(segment_piece[0], offset, block, 0)
        scores = (
            jnp.einsum("gqd,gkd->gqk", query, key_block, preferred_element_type=jnp.float32)
            * factor
        )
        key_places = offset + jnp.arange(block, dtype=jnp.int32)
        keep = (segment_block[None, :] == query_segments[:, None]) & (
            key_places[None, :] <= query_places[:, None]
        )
        block_top = jnp.max(jnp.where(keep[None], scores, jnp.float32(-1e30)), axis=2)
        newer = jnp.maximum(running, block_top)
        weights = jnp.where(keep[None], jnp.exp(scores - newer[:, :, None]), jnp.float32(0.0))
        shrink = jnp.exp(running - newer)
        total = total * shrink + jnp.sum(weights, axis=2)
        gathered = gathered * shrink[:, :, None] + jnp.einsum(
            "gqk,gkd->gqd",
            weights,
            value_block.astype(jnp.float32),
            precision=lax.Precision.HIGHEST,
        )
        return ((newer, total, gathered), None)

    result, unused = lax.scan(inner, begin, jnp.arange(count // block, dtype=jnp.int32))
    running, total, gathered = result
    attended = (
        (gathered / total[:, :, None]).astype(jnp.bfloat16).reshape(local_heads, rows, head_size)
    )
    terms = jnp.einsum(
        "htd,hcd->tc",
        attended,
        lax.all_gather(out_weight, "batch", axis=1, tiled=True),
        preferred_element_type=jnp.float32,
    )
    return lax.psum_scatter(terms, "heads", scatter_dimension=1, tiled=True).astype(jnp.bfloat16)


def solution(mesh):
    batch, heads = mesh.shape["batch"], mesh.shape["heads"]

    def on_device(tokens, query_weight, keys, values, segment_ids, out_weight):
        rows, model = tokens.shape
        local_heads, depth, head_size = query_weight.shape
        wide = local_heads * head_size
        weights = 2 * model * wide
        activations = batch * rows * (depth + 3 * wide + depth)
        plan = move_activations if batch == heads == 4 and activations < weights else gather_weights
        return plan(tokens, query_weight, keys, values, segment_ids, out_weight)

    return jax.shard_map(
        on_device,
        mesh=mesh,
        in_specs=(
            P(("groups", "batch"), None),
            P("heads", "batch", None),
            P("heads", ("groups", "batch"), None),
            P("heads", ("groups", "batch"), None),
            P(("groups", "batch")),
            P("heads", "batch", None),
        ),
        out_specs=P(("groups", "batch"), "heads"),
        check_vma=False,
    )
```
